128 devices in a mesh: dp: 16 (over y, z), ctx: 8 (over x, core).
Axes of the slice: x: 4, y: 4, z: 4, core: 2. Of those that a mesh axis runs over, the one named last changes fastest.
Arguments:
- queries: bfloat16 [64, 8, 128, 4096], P('dp', 'ctx'), may hold values from -6 to 6
- key_rows: bfloat16 [64, 8, 128, 512], P('dp', 'ctx'), may hold values from -6 to 6
- bin_value_rows: bfloat16 [64, 8, 128, 512], P('dp', 'ctx'), may hold values from -6 to 6
- lengths: int32 [64, 3], P('dp'), may hold values from 1 to 1021, as said below
- routes: int32 [64, 1], replicated, may hold values from 0 to 15, as said below
Outputs:
- attended: bfloat16 [64, 8, 128, 4096], P('dp', 'ctx')
The draws below stay inside these ranges and needn't reach their ends.
Inputs may be any that keep to these rules, and one draw needn't show every extreme that they name: `lengths`: every bin has a prompt of 2 or more positions and chosen and rejected responses of 1 or more; the three sum to at most 1024, with equality in some bin of every row. `routes`: rows are the aligned blocks of 4 bins. Each row sends its 4 bins to 4 different destination rows, and every destination row receives exactly 4 bins.
All inputs are finite; a program needn't handle non-finite values.
Results may differ from the reference program's by a relative error of at most 0.0039.
Values may be sent and summed in bfloat16 or wider, within the bound.
No kernel may reach another device: no remote copies, remote signals or barrier semaphores. Data moves between devices by JAX's collectives and lax.ppermute only.
A program may use at most 128 MiB of HBM per device.

```python
import math
import jax
import jax.numpy as jnp
from jax import lax

QUERY_HEADS = 32
KEY_VALUE_HEADS = 4
HEAD_SIZE = 128
BIN_POSITIONS = 128
ROW_PAIR_BINS = 4
TOTAL_BINS = 64
N_DP = 16
N_CTX = 8


def pair_lengths(key):
    position_span = N_CTX * BIN_POSITIONS
    item_count = N_DP * ROW_PAIR_BINS
    first_key, second_key, third_key, fourth_key = jax.random.split(jax.random.fold_in(key, 501), 4)
    prompt = jax.random.randint(first_key, (item_count,), 2, position_span // 2 + 1)
    rest = position_span - prompt
    chosen = jax.random.randint(second_key, (item_count,), 1, rest)
    left = rest - chosen
    rejected_free = jax.random.randint(third_key, (item_count,), 1, left + 1)
    picked = jax.random.randint(fourth_key, (N_DP,), 0, ROW_PAIR_BINS)
    full = jnp.arange(item_count, dtype=jnp.int32) % ROW_PAIR_BINS == jnp.repeat(picked, ROW_PAIR_BINS)
    rejected = jnp.where(full, left, rejected_free)
    first_bin = jnp.arange(item_count, dtype=jnp.int32) == 0
    prompt = jnp.where(first_bin, 2, prompt)
    chosen = jnp.where(first_bin, 1, chosen)
    rejected = jnp.where(first_bin, position_span - 3, rejected)
    return jnp.stack([prompt, chosen, rejected], axis=1).astype(jnp.int32)


def draw_lengths(key, part):
    return pair_lengths(key)


def draw_routes(key, part):
    key = jax.random.fold_in(key, 41)
    sigma_key, tau_key, row_key = jax.random.split(key, 3)
    sigma = jax.random.permutation(sigma_key, N_DP).astype(jnp.int32)
    tau = jax.random.permutation(tau_key, N_DP).astype(jnp.int32)
    shuffles = jax.vmap(lambda k: jax.random.permutation(k, ROW_PAIR_BINS))(jax.random.split(row_key, N_DP)).astype(jnp.int32)
    spots = (tau[:, None] + shuffles) % N_DP
    return sigma[spots].reshape(N_DP * ROW_PAIR_BINS, 1).astype(jnp.int32)


def draw_queries(key, part):
    key = jax.random.fold_in(key, 11)
    array_shape = (N_DP * ROW_PAIR_BINS, N_CTX, BIN_POSITIONS, QUERY_HEADS * HEAD_SIZE)
    base = jnp.clip(jax.random.normal(key, array_shape, jnp.float32), -6.0, 6.0)
    return base.astype(jnp.bfloat16)


def draw_key_rows(key, part):
    key = jax.random.fold_in(key, 23)
    array_shape = (N_DP * ROW_PAIR_BINS, N_CTX, BIN_POSITIONS, KEY_VALUE_HEADS * HEAD_SIZE)
    base = jnp.clip(jax.random.normal(key, array_shape, jnp.float32), -6.0, 6.0)
    return base.astype(jnp.bfloat16)


def steps_of(own_key, extent, pieces, low, high):
    def one(axis_at, shards_of):
        heights = jax.random.uniform(jax.random.fold_in(jax.random.fold_in(own_key, 6), axis_at), (shards_of,), jnp.float32, low / len(pieces), high / len(pieces))
        return jnp.repeat(jnp.exp(heights), extent[axis_at] // shards_of).reshape((-1,) + (1,) * (len(extent) - axis_at - 1))

    factor_of = one(*pieces[0])
    for cut in pieces[1:]:
        factor_of = factor_of * one(*cut)
    return factor_of


def bell_draw(key, dims, spread, limit, pieces=(), held_as=jnp.bfloat16):
    result = spread * jax.random.normal(key, dims, jnp.float32)
    if pieces:
        result = result * steps_of(key, dims, pieces, -0.22, 0.18)
    return jnp.clip(result, -limit, limit).astype(held_as)


def setup_inputs(seed: int = 0) -> dict:
    key_of = jax.random.split(jax.random.key(seed), 6)
    return {
        "queries": draw_queries(jax.random.fold_in(key_of[5], 71), 0),
        "key_rows": draw_key_rows(jax.random.fold_in(key_of[5], 71), 0),
        "bin_value_rows": bell_draw(key_of[2], (TOTAL_BINS, N_CTX, BIN_POSITIONS, KEY_VALUE_HEADS * HEAD_SIZE), 1.0, 6.0, ((0, 16), (1, 8))),
        "lengths": draw_lengths(jax.random.fold_in(key_of[5], 71), 0),
        "routes": draw_routes(jax.random.fold_in(key_of[5], 71), 0),
    }


def token_roles(lengths, positions):
    prompt = lengths[:, 0:1]
    chosen_len = lengths[:, 1:2]
    rejected_len = lengths[:, 2:3]
    places = positions[None, :]
    live = places < prompt + chosen_len + rejected_len
    chosen = (places >= prompt) & (places < prompt + chosen_len)
    rejected = (places >= prompt + chosen_len) & live
    return (live, chosen, rejected)

def visibility(lengths, query_pos, key_pos):
    live_q, chosen_q, reject_q = token_roles(lengths, query_pos)
    live_k, chosen_k, reject_k = token_roles(lengths, key_pos)
    causal = key_pos[None, None, :] <= query_pos[None, :, None]
    cross = chosen_q[:, :, None] & reject_k[:, None, :] | reject_q[:, :, None] & chosen_k[:, None, :]
    seen = causal & live_q[:, :, None] & live_k[:, None, :] & jnp.logical_not(cross)
    itself = jnp.logical_not(live_q)[:, :, None] & (key_pos[None, None, :] == query_pos[None, :, None])
    return (seen | itself, live_q)

def reference(queries, key_rows, bin_value_rows, lengths, routes):
    position_span = N_CTX * BIN_POSITIONS
    head_groups = QUERY_HEADS // KEY_VALUE_HEADS
    positions = jnp.arange(position_span, dtype=jnp.int32)
    scale_factor = 1.0 / math.sqrt(HEAD_SIZE)

    def one_bin(item):
        query_bin_rows, key_bin_rows, value_bin_rows, len_bin = item
        query_heads = query_bin_rows.reshape(position_span, KEY_VALUE_HEADS, head_groups, HEAD_SIZE).astype(jnp.float32)
        key_heads = key_bin_rows.reshape(position_span, KEY_VALUE_HEADS, HEAD_SIZE).astype(jnp.float32)
        value_heads = value_bin_rows.reshape(position_span, KEY_VALUE_HEADS, HEAD_SIZE).astype(jnp.float32)
        scores = jnp.einsum('qhgd,khd->hgqk', query_heads, key_heads) * scale_factor
        seen, live_q = visibility(len_bin[None, :], positions, positions)
        seen_b = seen[0][None, None]
        top = lax.optimization_barrier(jnp.max(jnp.where(seen_b, scores, -1e+30), axis=-1, keepdims=True))
        weights = jnp.where(seen_b, jnp.exp(scores - top), 0.0)
        total = lax.optimization_barrier(jnp.sum(weights, axis=-1))
        rounded = weights.astype(jnp.bfloat16).astype(jnp.float32)
        mixed = jnp.einsum('hgqk,khd->qhgd', rounded, value_heads)
        mixed = mixed / jnp.transpose(total, (2, 0, 1))[..., None]
        mixed = jnp.where(live_q[0][:, None, None, None], mixed, 0.0)
        return mixed.astype(jnp.bfloat16).reshape(N_CTX, BIN_POSITIONS, QUERY_HEADS * HEAD_SIZE)
    bin_out = lax.map(one_bin, (queries, key_rows, bin_value_rows, lengths))
    flat = routes[:, 0]
    order = jnp.arange(N_DP * ROW_PAIR_BINS, dtype=jnp.int32)
    earlier = (flat[:, None] == flat[None, :]) & (order[None, :] < order[:, None])
    placed = lax.optimization_barrier(jnp.sum(earlier.astype(jnp.int32), axis=1))
    index = (flat * ROW_PAIR_BINS + placed).astype(jnp.int32)
    attended = jnp.zeros((N_DP * ROW_PAIR_BINS, N_CTX, BIN_POSITIONS, QUERY_HEADS * HEAD_SIZE), jnp.bfloat16)
    return attended.at[index].set(bin_out)
```

```python
import functools
import math

import jax
import jax.numpy as jnp
from jax import lax
from jax.experimental import pallas as pl
from jax.experimental.pallas import tpu as pltpu
from jax.sharding import PartitionSpec as P

BINS = 4
ROWS = 16
CHIPS = 4
WIDTH = 128
HEAD = 128
GROUP = 8
PIECE = 16
PARTS = WIDTH // PIECE
HALF = GROUP // 2
NEG = -1e30
BF16 = jnp.bfloat16


def blocks(count):
    return jax.ShapeDtypeStruct((ROWS, count, PIECE, HEAD), BF16)


def pack_kernel(lengths, q_ref, k_ref, v_ref, u_ref, q_buf, k_buf, v_buf, u_buf, in_sems, out_sems):
    def arrive(b):
        wide, narrow = pl.ds(0, GROUP * HEAD), pl.ds(0, HEAD)
        return [
            pltpu.make_async_copy(q_ref.at[b, 0, :, wide], q_buf.at[b], in_sems.at[0, b]),
            pltpu.make_async_copy(k_ref.at[b, 0, :, narrow], k_buf.at[b], in_sems.at[1, b]),
            pltpu.make_async_copy(v_ref.at[b, 0, :, narrow], v_buf.at[b], in_sems.at[2, b]),
        ]

    def leave(i):
        part = pl.ds(i * HALF, HALF if i < BINS else BINS + 1)
        return pltpu.make_async_copy(u_buf.at[:, part], u_ref.at[:, part], out_sems.at[i])

    for b in range(BINS):
        for copy in arrive(b):
            copy.start()
    lane = lax.broadcasted_iota(jnp.int32, (PIECE, HEAD), 1)
    digits = jnp.zeros((PIECE, HEAD), jnp.int32)
    for i in range(3 * BINS):
        digits = jnp.where(lane == i, lengths[i] // 32, digits)
        digits = jnp.where(lane == 3 * BINS + i, lengths[i] % 32, digits)
    digits = digits.astype(jnp.float32).astype(BF16)
    for b in range(BINS):
        for copy in arrive(b):
            copy.wait()
        for j in range(ROWS):
            rows = pl.ds((j // 2) * PIECE, PIECE)
            for n in range(HALF):
                u_buf[j, b * HALF + n] = q_buf[b, rows, pl.ds(((j % 2) * HALF + n) * HEAD, HEAD)]
            u_buf[j, BINS * HALF + b] = (k_buf if j % 2 == 0 else v_buf)[b, rows]
            if b == 0:
                u_buf[j, BINS * HALF + BINS] = digits
        leave(b).start()
    leave(BINS).start()
    for i in range(BINS + 1):
        leave(i).wait()


def pack(lengths, queries, key_rows, value_rows):
    hbm = pl.BlockSpec(memory_space=pltpu.HBM)
    count = BINS * HALF + BINS + 1
    return pl.pallas_call(
        pack_kernel,
        grid_spec=pltpu.PrefetchScalarGridSpec(
            num_scalar_prefetch=1,
            grid=(),
            in_specs=[hbm] * 3,
            out_specs=hbm,
            scratch_shapes=[
                pltpu.VMEM((BINS, WIDTH, GROUP * HEAD), BF16),
                pltpu.VMEM((BINS, WIDTH, HEAD), BF16),
                pltpu.VMEM((BINS, WIDTH, HEAD), BF16),
                pltpu.VMEM((ROWS, count, PIECE, HEAD), BF16),
                pltpu.SemaphoreType.DMA((3, BINS)),
                pltpu.SemaphoreType.DMA((BINS + 1,)),
            ],
        ),
        out_shape=blocks(count),
        cost_estimate=pl.CostEstimate(flops=0, bytes_accessed=4 << 20, transcendentals=0),
        name="pack",
    )(lengths, queries, key_rows, value_rows)


def attend_kernel(from_pieces, to_pieces, scalars, q_ref, *refs):
    kv_refs, (out_ref, buffer, sems) = refs[: 2 * CHIPS], refs[2 * CHIPS :]
    item, head_at = pl.program_id(0), pl.program_id(1)
    ctx = scalars[3 * BINS]
    chip, core = ctx // 2, ctx % 2
    prompt = scalars[3 * item]
    split = prompt + scalars[3 * item + 1]
    end = split + scalars[3 * item + 2]
    start = ctx * WIDTH
    factor = math.log2(math.e) / math.sqrt(HEAD)

    def copy(i, b):
        return pltpu.make_async_copy(kv_refs[i].at[:, b], buffer.at[i, b], sems.at[i, b])

    @pl.when((item == 0) & (head_at == 0))
    def _():
        for b in range(BINS):
            for i in range(2 * CHIPS):

                @pl.when(i // 2 <= chip)
                def _(i=i, b=b):
                    copy(i, b).start()

    @pl.when(head_at == 0)
    def _():
        for i in range(2 * CHIPS):

            @pl.when(i // 2 <= chip)
            def _(i=i):
                copy(i, item).wait()

    def read_head(head):
        if not from_pieces:
            return q_ref[0, 0, :, pl.ds(head * HEAD, HEAD)]
        return jnp.concatenate([q_ref[2 * r + head // HALF, head % HALF] for r in range(PARTS)], axis=0)

    def write_head(head, rows):
        if to_pieces:
            for r in range(PARTS):
                out_ref[2 * r + head // HALF, head % HALF] = rows[r * PIECE : (r + 1) * PIECE]
        else:
            out_ref[0, 0, :, pl.ds(head * HEAD, HEAD)] = rows

    def attend(chips):
        keys = jnp.concatenate([buffer[i, item, 2 * head_at] for i in range(2 * chips)], axis=0)
        values = jnp.concatenate([buffer[i, item, 2 * head_at + 1] for i in range(2 * chips)], axis=0)
        t = start + lax.broadcasted_iota(jnp.int32, (WIDTH, WIDTH), 0)
        biases = []
        for i in range(2 * chips):
            origin = 2 * (chip - i // 2) + (core if i % 2 == 0 else 1 - core)
            u = origin * WIDTH + lax.broadcasted_iota(jnp.int32, (WIDTH, WIDTH), 1)
            hidden = (u > t) | ((t >= split) & (u >= prompt) & (u < split))
            biases.append(jnp.where(hidden, NEG, 0.0))
        bias = jnp.concatenate(biases, axis=1)
        live = (start + lax.broadcasted_iota(jnp.int32, (WIDTH, 1), 0)) < end
        bias = jnp.concatenate([bias, bias], axis=0)
        live = jnp.concatenate([live, live], axis=0)
        n = GROUP // 2
        qs = [jnp.concatenate([read_head(2 * i), read_head(2 * i + 1)], axis=0) for i in range(n)]
        scores = [lax.dot_general(q, keys, (((1,), (1,)), ((), ())), preferred_element_type=jnp.float32) + bias for q in qs]
        tops = [jnp.max(x, axis=1, keepdims=True) for x in scores]
        weights = [jnp.exp2((x - top) * factor) for x, top in zip(scores, tops)]
        wide = jnp.concatenate([values, jnp.ones_like(values)], axis=1)
        mixed = [jnp.dot(x.astype(BF16), wide, preferred_element_type=jnp.float32) for x in weights]
        for i in range(n):
            out = (mixed[i][:, :HEAD] * jnp.where(live, 1.0 / mixed[i][:, HEAD:], 0.0)).astype(BF16)
            write_head(2 * i, out[:WIDTH])
            write_head(2 * i + 1, out[WIDTH:])

    @pl.when(end <= start)
    def _():
        out_ref[...] = jnp.zeros_like(out_ref)

    for chips in range(1, CHIPS + 1):

        @pl.when((end > start) & (chip == chips - 1))
        def _(chips=chips):
            attend(chips)


def attend(scalars, q, kv, heads, q_spec, out_spec, out_shape, from_pieces, to_pieces, name):
    pairs = BINS * heads * GROUP * WIDTH * WIDTH * 2 * CHIPS
    return pl.pallas_call(
        functools.partial(attend_kernel, from_pieces, to_pieces),
        grid_spec=pltpu.PrefetchScalarGridSpec(
            num_scalar_prefetch=1,
            grid=(BINS, heads),
            in_specs=[q_spec] + [pl.BlockSpec(memory_space=pltpu.HBM)] * (2 * CHIPS),
            out_specs=out_spec,
            scratch_shapes=[
                pltpu.VMEM((2 * CHIPS, BINS, 2 * heads, WIDTH, HEAD), BF16),
                pltpu.SemaphoreType.DMA((2 * CHIPS, BINS)),
            ],
        ),
        out_shape=out_shape,
        cost_estimate=pl.CostEstimate(flops=4 * pairs * HEAD, bytes_accessed=heads * (4 << 20), transcendentals=pairs),
        compiler_params=pltpu.CompilerParams(vmem_limit_bytes=48 << 20),
        name=name,
    )(scalars, q, *kv)


def forward_kernel(sizes, at, bin_of, r_ref, *refs):
    u_ref, r_buf, u_buf, in_sem, out_sems = refs[-5:]
    arrive = pltpu.make_async_copy(r_ref.at[:, pl.ds(0, r_buf.shape[1])], r_buf, in_sem)
    arrive.start()
    arrive.wait()

    def leave(row):
        return pltpu.make_async_copy(u_buf.at[row], u_ref.at[row, pl.ds(at, u_buf.shape[1])], out_sems.at[row])

    for row in range(ROWS):
        for slot in range(BINS):
            b = bin_of[row * BINS + slot]
            base = 0
            for size in sizes:
                for n in range(size):
                    u_buf[row, base + slot * size + n] = r_buf[b // BINS, base + (b % BINS) * size + n]
                base += BINS * size
        leave(row).start()
    for row in range(ROWS):
        leave(row).wait()


def forward(bin_of, received, sizes, into, name):
    hbm = pl.BlockSpec(memory_space=pltpu.HBM)
    count = BINS * sum(sizes)
    at = 0 if into is None else into.shape[1] - count
    return pl.pallas_call(
        functools.partial(forward_kernel, sizes, at),
        grid_spec=pltpu.PrefetchScalarGridSpec(
            num_scalar_prefetch=1,
            grid=(),
            in_specs=[pl.BlockSpec(memory_space=pl.ANY)] + [hbm] * (0 if into is None else 1),
            out_specs=hbm,
            scratch_shapes=[
                pltpu.VMEM((ROWS, count, PIECE, HEAD), BF16),
                pltpu.VMEM((ROWS, count, PIECE, HEAD), BF16),
                pltpu.SemaphoreType.DMA,
                pltpu.SemaphoreType.DMA((ROWS,)),
            ],
        ),
        out_shape=blocks(count) if into is None else jax.ShapeDtypeStruct(into.shape, BF16),
        input_output_aliases={} if into is None else {2: 0},
        cost_estimate=pl.CostEstimate(flops=0, bytes_accessed=4 << 20, transcendentals=0),
        name=name,
    )(bin_of, received, *(() if into is None else (into,)))


def place_kernel(at, heads, column, r_ref, _, out_ref, r_buf, out_buf, in_sems, out_sems):
    size = HALF * heads

    def arrive(slot):
        return pltpu.make_async_copy(r_ref.at[:, pl.ds(at + slot * size, size)], r_buf.at[slot], in_sems.at[slot])

    def leave(slot):
        columns = pl.ds(column, heads * GROUP * HEAD)
        return pltpu.make_async_copy(out_buf.at[slot], out_ref.at[slot, 0, :, columns], out_sems.at[slot])

    for slot in range(BINS):
        arrive(slot).start()
    for slot in range(BINS):
        arrive(slot).wait()
        for j in range(ROWS):
            for n in range(size):
                head = (n // HALF) * GROUP + (j % 2) * HALF + n % HALF
                out_buf[slot, pl.ds((j // 2) * PIECE, PIECE), pl.ds(head * HEAD, HEAD)] = r_buf[slot, j, n]
        leave(slot).start()
    for slot in range(BINS):
        leave(slot).wait()


def place(received, at, heads, out, column, name):
    hbm = pl.BlockSpec(memory_space=pltpu.HBM)
    return pl.pallas_call(
        functools.partial(place_kernel, at, heads, column),
        in_specs=[pl.BlockSpec(memory_space=pl.ANY), hbm],
        out_specs=hbm,
        out_shape=jax.ShapeDtypeStruct(out.shape, out.dtype),
        scratch_shapes=[
            pltpu.VMEM((BINS, ROWS, HALF * heads, PIECE, HEAD), BF16),
            pltpu.VMEM((BINS, WIDTH, heads * GROUP * HEAD), BF16),
            pltpu.SemaphoreType.DMA((BINS,)),
            pltpu.SemaphoreType.DMA((BINS,)),
        ],
        input_output_aliases={1: 0},
        cost_estimate=pl.CostEstimate(flops=0, bytes_accessed=heads * (2 << 20), transcendentals=0),
        name=name,
    )(received, out)


def fetch(kv):
    pieces = [kv]
    for back in range(1, CHIPS):
        pairs = [(2 * x + core, 2 * (x + back) + core) for x in range(CHIPS - back) for core in range(2)]
        pieces.append(lax.ppermute(kv, "ctx", pairs))
    return pieces


def share(pieces):
    swap = [(c, c ^ 1) for c in range(2 * CHIPS)]
    return [p for piece in pieces for p in (piece, lax.ppermute(piece, "ctx", swap))]


def exchange(sent):
    return lax.all_to_all(sent, "dp", split_axis=0, concat_axis=0, tiled=True)


def shards(queries, key_rows, bin_value_rows, lengths, routes):
    my_row = lax.axis_index("dp")
    ctx = lax.axis_index("ctx").astype(jnp.int32)
    flat = routes[:, 0]
    order = jnp.arange(ROWS * BINS, dtype=jnp.int32)
    earlier = (flat[:, None] == flat[None, :]) & (order[None, :] < order[:, None])
    slot = flat * BINS + jnp.sum(earlier.astype(jnp.int32), axis=1)
    bin_of = jnp.sum(jnp.where(slot[None, :] == order[:, None], order[None, :], 0), axis=1).astype(jnp.int32)
    flat_lengths = lengths.reshape(-1)

    def key_value(heads):
        columns = [slice(h * HEAD, (h + 1) * HEAD) for h in heads]
        return jnp.stack([a[:, 0, :, c] for c in columns for a in (key_rows, bin_value_rows)])

    def query_spec(first):
        return pl.BlockSpec((1, 1, WIDTH, GROUP * HEAD), lambda b, h, s: (b, 0, 0, first + h))

    def piece_spec(first, heads):
        return pl.BlockSpec((ROWS, HALF, PIECE, HEAD), lambda b, h, s: (0, first + b * heads + h, 0, 0))

    near_a = fetch(key_value([1]))
    pieces_a = share(near_a)
    got_1 = exchange(pack(flat_lengths, queries, key_rows, bin_value_rows))

    kv_b, near_a[3] = lax.optimization_barrier((key_value([2, 3]), near_a[3]))
    near_b = fetch(kv_b)

    here = jnp.concatenate([flat_lengths, ctx[None]])
    second = attend(here, queries, pieces_a, 1, query_spec(1), piece_spec(0, 1), blocks(36), False, True, "attend_a")
    second = forward(bin_of, got_1, (HALF, 1), second, "forward_q")
    second, near_b = lax.optimization_barrier((second, near_b))
    got_2 = exchange(second)

    digits = got_1[:, 5 * BINS, 0, : 6 * BINS].astype(jnp.float32).astype(jnp.int32)
    all_lengths = (digits[:, : 3 * BINS] * 32 + digits[:, 3 * BINS :]).reshape(ROWS * BINS, 3)
    my_bins = lax.dynamic_slice_in_dim(bin_of, my_row * BINS, BINS)
    slot_lengths = jnp.sum(jnp.where(my_bins[:, None, None] == order[None, :, None], all_lengths[None], 0), axis=1)
    there = jnp.concatenate([slot_lengths.reshape(-1).astype(jnp.int32), ctx[None]])

    pieces_b = share(near_b)
    third = attend(here, queries, pieces_b, 2, query_spec(2), piece_spec(0, 2), blocks(48), False, True, "attend_b")
    third = forward(bin_of, got_2, (HALF,), third, "forward_a")
    third, there = lax.optimization_barrier((third, there))
    got_3 = exchange(third)

    kv_0 = jnp.transpose(got_2[:, 32:].reshape(PARTS, 2, BINS, PIECE, HEAD), (1, 2, 0, 3, 4))
    pieces_0 = share(fetch(kv_0.reshape(2, BINS, WIDTH, HEAD)))
    full = jax.ShapeDtypeStruct(queries.shape, BF16)
    out = attend(there, got_2, pieces_0, 1, piece_spec(4, 1), query_spec(0), full, True, False, "attend_0")

    fourth = forward(bin_of, got_3, (2 * HALF,), None, "forward_b")
    fourth, out = lax.optimization_barrier((fourth, out))
    got_4 = exchange(fourth)
    out = place(got_3, 32, 1, out, GROUP * HEAD, "place_a")
    return place(got_4, 0, 2, out, 2 * GROUP * HEAD, "place_b")


def solution(mesh):
    in_specs = (
        P("dp", "ctx", None, None),
        P("dp", "ctx", None, None),
        P("dp", "ctx", None, None),
        P("dp", None),
        P(),
    )
    out_specs = P("dp", "ctx", None, None)
    return jax.shard_map(shards, mesh=mesh, in_specs=in_specs, out_specs=out_specs, check_vma=False)
```

```python
import functools
import math

import jax
import jax.numpy as jnp
from jax import lax
from jax.experimental import pallas as pl
from jax.experimental.pallas import tpu as pltpu
from jax.sharding import PartitionSpec as P

BINS = 4
ROWS = 16
CHIPS = 4
WIDTH = 128
HEAD = 128
GROUP = 8
PIECE = 16
PARTS = WIDTH // PIECE
HALF = GROUP // 2
NEG = -1e30
BF16 = jnp.bfloat16
VMEM_LIMIT = 40 << 20


def blocks(count):
    return pltpu.HBM((ROWS, count, PIECE, HEAD), BF16)


def pack_kernel(lengths, q_ref, k_ref, v_ref, u_ref, q_buf, k_buf, v_buf, u_buf, in_sems, out_sems):
    def arrive(b):
        wide, narrow = pl.ds(0, GROUP * HEAD), pl.ds(0, HEAD)
        return [
            pltpu.make_async_copy(q_ref.at[b, 0, :, wide], q_buf.at[b], in_sems.at[0, b]),
            pltpu.make_async_copy(k_ref.at[b, 0, :, narrow], k_buf.at[b], in_sems.at[1, b]),
            pltpu.make_async_copy(v_ref.at[b, 0, :, narrow], v_buf.at[b], in_sems.at[2, b]),
        ]

    def leave(i):
        part = pl.ds(i * HALF, HALF if i < BINS else BINS + 1)
        return pltpu.make_async_copy(u_buf.at[:, part], u_ref.at[:, part], out_sems.at[i])

    for b in range(BINS):
        for copy in arrive(b):
            copy.start()
    lane = lax.broadcasted_iota(jnp.int32, (PIECE, HEAD), 1)
    digits = jnp.zeros((PIECE, HEAD), jnp.int32)
    for i in range(3 * BINS):
        length = lengths[i // 3, i % 3]
        digits = jnp.where(lane == i, length // 32, digits)
        digits = jnp.where(lane == 3 * BINS + i, length % 32, digits)
    digits = digits.astype(jnp.float32).astype(BF16)
    for b in range(BINS):
        for copy in arrive(b):
            copy.wait()
        for j in range(ROWS):
            rows = pl.ds((j // 2) * PIECE, PIECE)
            for n in range(HALF):
                u_buf[j, b * HALF + n] = q_buf[b, rows, pl.ds(((j % 2) * HALF + n) * HEAD, HEAD)]
            u_buf[j, BINS * HALF + b] = (k_buf if j % 2 == 0 else v_buf)[b, rows]
            if b == 0:
                u_buf[j, BINS * HALF + BINS] = digits
        leave(b).start()
    leave(BINS).start()
    for i in range(BINS + 1):
        leave(i).wait()


def pack(lengths, queries, key_rows, value_rows):
    hbm = pl.BlockSpec(memory_space=pltpu.HBM)
    count = BINS * HALF + BINS + 1
    return pl.pallas_call(
        pack_kernel,
        grid_spec=pltpu.PrefetchScalarGridSpec(
            num_scalar_prefetch=1,
            grid=(),
            in_specs=[hbm] * 3,
            out_specs=hbm,
            scratch_shapes=[
                pltpu.VMEM((BINS, WIDTH, GROUP * HEAD), BF16),
                pltpu.VMEM((BINS, WIDTH, HEAD), BF16),
                pltpu.VMEM((BINS, WIDTH, HEAD), BF16),
                pltpu.VMEM((ROWS, count, PIECE, HEAD), BF16),
                pltpu.SemaphoreType.DMA((3, BINS)),
                pltpu.SemaphoreType.DMA((BINS + 1,)),
            ],
        ),
        out_shape=blocks(count),
        cost_estimate=pl.CostEstimate(flops=0, bytes_accessed=4 << 20, transcendentals=0),
        compiler_params=pltpu.CompilerParams(vmem_limit_bytes=VMEM_LIMIT),
        name="pack",
    )(lengths, *(pltpu.with_memory_space_constraint(a, pltpu.HBM) for a in (queries, key_rows, value_rows)))


def attend_kernel(head_at, from_pieces, to_pieces, lengths, place, q_ref, *refs):
    kv_refs, (out_ref, buffer, sems) = refs[: 2 * CHIPS], refs[-3:]
    item = pl.program_id(0)
    ctx = place[0]
    chip, core = ctx // 2, ctx % 2
    prompt = lengths[item, 0]
    split = prompt + lengths[item, 1]
    end = split + lengths[item, 2]
    start = ctx * WIDTH
    factor = math.log2(math.e) / math.sqrt(HEAD)

    def copy(i, b):
        return pltpu.make_async_copy(kv_refs[i].at[pl.ds(2 * head_at, 2), b], buffer.at[i, b], sems.at[i, b])

    @pl.when(item == 0)
    def _():
        for b in range(BINS):
            for i in range(2 * CHIPS):

                @pl.when(i // 2 <= chip)
                def _(i=i, b=b):
                    copy(i, b).start()

    for i in range(2 * CHIPS):

        @pl.when(i // 2 <= chip)
        def _(i=i):
            copy(i, item).wait()

    def read_head(head):
        if not from_pieces:
            return q_ref[0, 0, :, pl.ds(head * HEAD, HEAD)]
        return jnp.concatenate([q_ref[2 * r + head // HALF, head % HALF] for r in range(PARTS)], axis=0)

    def write_head(head, rows):
        if to_pieces:
            for r in range(PARTS):
                out_ref[2 * r + head // HALF, head % HALF] = rows[r * PIECE : (r + 1) * PIECE]
        else:
            out_ref[0, 0, :, pl.ds(head * HEAD, HEAD)] = rows

    def attend(chips):
        keys = jnp.concatenate([buffer[i, item, 0] for i in range(2 * chips)], axis=0)
        values = jnp.concatenate([buffer[i, item, 1] for i in range(2 * chips)], axis=0)
        t = start + lax.broadcasted_iota(jnp.int32, (WIDTH, WIDTH), 0)
        biases = []
        for i in range(2 * chips):
            origin = 2 * (chip - i // 2) + (core if i % 2 == 0 else 1 - core)
            u = origin * WIDTH + lax.broadcasted_iota(jnp.int32, (WIDTH, WIDTH), 1)
            hidden = (u > t) | ((t >= split) & (u >= prompt) & (u < split))
            biases.append(jnp.where(hidden, NEG, 0.0))
        bias = jnp.concatenate(biases, axis=1)
        live = (start + lax.broadcasted_iota(jnp.int32, (WIDTH, 1), 0)) < end
        bias = jnp.concatenate([bias, bias], axis=0)
        live = jnp.concatenate([live, live], axis=0)
        n = GROUP // 2
        qs = [jnp.concatenate([read_head(2 * i), read_head(2 * i + 1)], axis=0) for i in range(n)]
        scores = [lax.dot_general(q, keys, (((1,), (1,)), ((), ())), preferred_element_type=jnp.float32) + bias for q in qs]
        tops = [jnp.max(x, axis=1, keepdims=True) for x in scores]
        weights = [jnp.exp2((x - top) * factor) for x, top in zip(scores, tops)]
        wide = jnp.concatenate([values, jnp.ones_like(values)], axis=1)
        mixed = [jnp.dot(x.astype(BF16), wide, preferred_element_type=jnp.float32) for x in weights]
        for i in range(n):
            out = (mixed[i][:, :HEAD] * jnp.where(live, 1.0 / mixed[i][:, HEAD:], 0.0)).astype(BF16)
            write_head(2 * i, out[:WIDTH])
            write_head(2 * i + 1, out[WIDTH:])

    @pl.when(end <= start)
    def _():
        out_ref[...] = jnp.zeros_like(out_ref)

    for chips in range(1, CHIPS + 1):

        @pl.when((end > start) & (chip == chips - 1))
        def _(chips=chips):
            attend(chips)


def attend(lengths, place, q, kv, q_spec, out_spec, out_shape, name, from_pieces=False, to_pieces=True, into=None, head_at=0, weight=1):
    hbm = pl.BlockSpec(memory_space=pltpu.HBM)
    pairs = BINS * GROUP * WIDTH * WIDTH * 2 * CHIPS
    return pl.pallas_call(
        functools.partial(attend_kernel, head_at, from_pieces, to_pieces),
        grid_spec=pltpu.PrefetchScalarGridSpec(
            num_scalar_prefetch=2,
            grid=(BINS,),
            in_specs=[q_spec] + [hbm] * (2 * CHIPS + (0 if into is None else 1)),
            out_specs=out_spec,
            scratch_shapes=[
                pltpu.VMEM((2 * CHIPS, BINS, 2, WIDTH, HEAD), BF16),
                pltpu.SemaphoreType.DMA((2 * CHIPS, BINS)),
            ],
        ),
        out_shape=out_shape,
        input_output_aliases={} if into is None else {3 + 2 * CHIPS: 0},
        cost_estimate=pl.CostEstimate(flops=int(weight * 20 * pairs * HEAD), bytes_accessed=4 << 20, transcendentals=pairs),
        compiler_params=pltpu.CompilerParams(vmem_limit_bytes=VMEM_LIMIT),
        name=name,
    )(lengths, place, *(pltpu.with_memory_space_constraint(a, pltpu.HBM) for a in (q, *kv)), *(() if into is None else (into,)))


def forward_kernel(sizes, at, bin_of, r_ref, *refs):
    u_ref, u_buf, sems = refs[-3:]

    def leave(row):
        return pltpu.make_async_copy(u_buf.at[row], u_ref.at[row, pl.ds(at, u_buf.shape[1])], sems.at[row])

    for row in range(ROWS):
        for slot in range(BINS):
            b = bin_of[row * BINS + slot]
            base = 0
            for size in sizes:
                for n in range(size):
                    u_buf[row, base + slot * size + n] = r_ref[b // BINS, base + (b % BINS) * size + n]
                base += BINS * size
        leave(row).start()
    for row in range(ROWS):
        leave(row).wait()


def forward(bin_of, received, sizes, into, name):
    hbm = pl.BlockSpec(memory_space=pltpu.HBM)
    count = BINS * sum(sizes)
    at = 0 if into is None else into.shape[1] - count
    return pl.pallas_call(
        functools.partial(forward_kernel, sizes, at),
        grid_spec=pltpu.PrefetchScalarGridSpec(
            num_scalar_prefetch=1,
            grid=(),
            in_specs=[pl.BlockSpec(memory_space=pltpu.VMEM)] + [hbm] * (0 if into is None else 1),
            out_specs=hbm,
            scratch_shapes=[pltpu.VMEM((ROWS, count, PIECE, HEAD), BF16), pltpu.SemaphoreType.DMA((ROWS,))],
        ),
        out_shape=blocks(count) if into is None else blocks(into.shape[1]),
        input_output_aliases={} if into is None else {2: 0},
        cost_estimate=pl.CostEstimate(flops=0, bytes_accessed=4 << 20, transcendentals=0),
        compiler_params=pltpu.CompilerParams(vmem_limit_bytes=VMEM_LIMIT),
        name=name,
    )(bin_of, pltpu.with_memory_space_constraint(received, pltpu.VMEM), *(() if into is None else (into,)))


def place_kernel(at, column, r_ref, _, out_ref, out_buf, sems):
    heads = len(at)

    def leave(slot):
        columns = pl.ds(column, heads * GROUP * HEAD)
        return pltpu.make_async_copy(out_buf.at[slot], out_ref.at[slot, 0, :, columns], sems.at[slot])

    for slot in range(BINS):
        for j in range(ROWS):
            for n in range(HALF * heads):
                head = (n // HALF) * GROUP + (j % 2) * HALF + n % HALF
                rows, columns = pl.ds((j // 2) * PIECE, PIECE), pl.ds(head * HEAD, HEAD)
                out_buf[slot, rows, columns] = r_ref[j, at[n // HALF] + slot * HALF + n % HALF]
        leave(slot).start()
    for slot in range(BINS):
        leave(slot).wait()


def place(received, at, out, column, name):
    hbm = pl.BlockSpec(memory_space=pltpu.HBM)
    heads = len(at)
    return pl.pallas_call(
        functools.partial(place_kernel, at, column),
        in_specs=[pl.BlockSpec(memory_space=pltpu.VMEM), hbm],
        out_specs=hbm,
        out_shape=jax.ShapeDtypeStruct(out.shape, out.dtype),
        scratch_shapes=[
            pltpu.VMEM((BINS, WIDTH, heads * GROUP * HEAD), BF16),
            pltpu.SemaphoreType.DMA((BINS,)),
        ],
        input_output_aliases={1: 0},
        cost_estimate=pl.CostEstimate(flops=0, bytes_accessed=heads * (2 << 20), transcendentals=0),
        compiler_params=pltpu.CompilerParams(vmem_limit_bytes=VMEM_LIMIT),
        name=name,
    )(pltpu.with_memory_space_constraint(received, pltpu.VMEM), out)


def fetch(kv):
    pieces = [kv]
    for back in range(1, CHIPS):
        pairs = [(c, (c + 2 * back) % (2 * CHIPS)) for c in range(2 * CHIPS)]
        pieces.append(lax.ppermute(kv, "ctx", pairs))
    return pieces


def share(pieces):
    swap = [(c, c ^ 1) for c in range(2 * CHIPS)]
    return [p for piece in pieces for p in (piece, lax.ppermute(piece, "ctx", swap))]


def exchange(sent):
    return lax.all_to_all(sent, "dp", split_axis=0, concat_axis=0, tiled=True)


def shards(queries, key_rows, bin_value_rows, lengths, routes):
    my_row = lax.axis_index("dp")
    ctx = lax.axis_index("ctx").astype(jnp.int32)[None]
    flat = routes[:, 0]
    order = jnp.arange(ROWS * BINS, dtype=jnp.int32)
    earlier = (flat[:, None] == flat[None, :]) & (order[None, :] < order[:, None])
    slot = flat * BINS + jnp.sum(earlier.astype(jnp.int32), axis=1)
    bin_of = jnp.sum(jnp.where(slot[None, :] == order[:, None], order[None, :], 0), axis=1).astype(jnp.int32)

    def key_value(heads, near=None):
        k, v = key_rows, bin_value_rows
        if near is not None:
            k, v, near[CHIPS - 1] = lax.optimization_barrier((k, v, near[CHIPS - 1]))
        columns = [slice(head * HEAD, (head + 1) * HEAD) for head in heads]
        return jnp.stack([a[:, 0, :, c] for c in columns for a in (k, v)])

    def query_spec(head):
        return pl.BlockSpec((1, 1, WIDTH, GROUP * HEAD), lambda b, *_: (b, 0, 0, head))

    def piece_spec(group):
        return pl.BlockSpec((ROWS, HALF, PIECE, HEAD), lambda b, *_: (0, group * BINS + b, 0, 0))

    near_1 = fetch(key_value([1]))
    got_1 = exchange(pack(lengths, queries, key_rows, bin_value_rows))
    near_23 = fetch(key_value([2, 3], near_1))

    second = attend(lengths, ctx, queries, share(near_1), query_spec(1), piece_spec(0), blocks(36), "attend_1")
    second = forward(bin_of, got_1, (HALF, 1), second, "forward_0")
    got_2 = exchange(second)
    near_23[1:], _ = lax.optimization_barrier((near_23[1:], second))

    digits = got_1[:, 5 * BINS, 0, : 6 * BINS].astype(jnp.float32).astype(jnp.int32)
    all_lengths = (digits[:, : 3 * BINS] * 32 + digits[:, 3 * BINS :]).reshape(ROWS * BINS, 3)
    my_bins = lax.dynamic_slice_in_dim(bin_of, my_row * BINS, BINS)
    slot_lengths = jnp.sum(jnp.where(my_bins[:, None, None] == order[None, :, None], all_lengths[None], 0), axis=1).astype(jnp.int32)

    pieces_23 = share(near_23)
    third = attend(lengths, ctx, queries, pieces_23, query_spec(2), piece_spec(0), blocks(48), "attend_2", weight=3)
    third = attend(lengths, ctx, queries, pieces_23, query_spec(3), piece_spec(1), blocks(48), "attend_3", into=third, head_at=1, weight=3)
    third = forward(bin_of, got_2, (HALF,), third, "forward_1")
    third, slot_lengths = lax.optimization_barrier((third, slot_lengths))
    got_3 = exchange(third)

    kv_0 = jnp.transpose(got_2[:, 32:].reshape(PARTS, 2, BINS, PIECE, HEAD), (1, 2, 0, 3, 4))
    pieces_0 = share(fetch(kv_0.reshape(2, BINS, WIDTH, HEAD)))
    full = jax.ShapeDtypeStruct(queries.shape, BF16)
    out = attend(slot_lengths, ctx, got_2, pieces_0, piece_spec(1), query_spec(0), full, "attend_0", True, False)

    fourth = forward(bin_of, got_3, (HALF, HALF), None, "forward_23")
    fourth, out = lax.optimization_barrier((fourth, out))
    got_4 = exchange(fourth)
    out = place(got_3, (32,), out, GROUP * HEAD, "place_1")
    return place(got_4, (0, 16), out, 2 * GROUP * HEAD, "place_23")


def solution(mesh):
    in_specs = (
        P("dp", "ctx", None, None),
        P("dp", "ctx", None, None),
        P("dp", "ctx", None, None),
        P("dp", None),
        P(),
    )
    out_specs = P("dp", "ctx", None, None)
    return jax.shard_map(shards, mesh=mesh, in_specs=in_specs, out_specs=out_specs, check_vma=False)
```

```python
import functools
import math

import jax
import jax.numpy as jnp
from jax import lax
from jax.experimental import pallas as pl
from jax.experimental.pallas import tpu as pltpu
from jax.sharding import PartitionSpec as P

BINS = 4
ROWS = 16
CHIPS = 4
WIDTH = 128
HEAD = 128
GROUP = 8
PIECE = 16
PARTS = WIDTH // PIECE
HALF = GROUP // 2
NEG = -1e30
BF16 = jnp.bfloat16
VMEM_LIMIT = 40 << 20


def blocks(count):
    return pltpu.HBM((ROWS, count, PIECE, HEAD), BF16)


def pack_kernel(lengths, q_ref, k_ref, v_ref, u_ref, q_buf, k_buf, v_buf, u_buf, in_sems, out_sems):
    def arrive(b):
        wide, narrow = pl.ds(0, GROUP * HEAD), pl.ds(0, HEAD)
        return [
            pltpu.make_async_copy(q_ref.at[b, 0, :, wide], q_buf.at[b], in_sems.at[0, b]),
            pltpu.make_async_copy(k_ref.at[b, 0, :, narrow], k_buf.at[b], in_sems.at[1, b]),
            pltpu.make_async_copy(v_ref.at[b, 0, :, narrow], v_buf.at[b], in_sems.at[2, b]),
        ]

    def leave(i):
        part = pl.ds(i * HALF, HALF if i < BINS else BINS + 1)
        return pltpu.make_async_copy(u_buf.at[:, part], u_ref.at[:, part], out_sems.at[i])

    for b in range(BINS):
        for copy in arrive(b):
            copy.start()
    lane = lax.broadcasted_iota(jnp.int32, (PIECE, HEAD), 1)
    digits = jnp.zeros((PIECE, HEAD), jnp.int32)
    for i in range(3 * BINS):
        length = lengths[i // 3, i % 3]
        digits = jnp.where(lane == i, length // 32, digits)
        digits = jnp.where(lane == 3 * BINS + i, length % 32, digits)
    digits = digits.astype(jnp.float32).astype(BF16)
    for b in range(BINS):
        for copy in arrive(b):
            copy.wait()
        for j in range(ROWS):
            rows = pl.ds((j // 2) * PIECE, PIECE)
            for n in range(HALF):
                u_buf[j, b * HALF + n] = q_buf[b, rows, pl.ds(((j % 2) * HALF + n) * HEAD, HEAD)]
            u_buf[j, BINS * HALF + b] = (k_buf if j % 2 == 0 else v_buf)[b, rows]
            if b == 0:
                u_buf[j, BINS * HALF + BINS] = digits
        leave(b).start()
    leave(BINS).start()
    for i in range(BINS + 1):
        leave(i).wait()


def pack(lengths, queries, key_rows, value_rows):
    hbm = pl.BlockSpec(memory_space=pltpu.HBM)
    count = BINS * HALF + BINS + 1
    return pl.pallas_call(
        pack_kernel,
        grid_spec=pltpu.PrefetchScalarGridSpec(
            num_scalar_prefetch=1,
            grid=(),
            in_specs=[hbm] * 3,
            out_specs=hbm,
            scratch_shapes=[
                pltpu.VMEM((BINS, WIDTH, GROUP * HEAD), BF16),
                pltpu.VMEM((BINS, WIDTH, HEAD), BF16),
                pltpu.VMEM((BINS, WIDTH, HEAD), BF16),
                pltpu.VMEM((ROWS, count, PIECE, HEAD), BF16),
                pltpu.SemaphoreType.DMA((3, BINS)),
                pltpu.SemaphoreType.DMA((BINS + 1,)),
            ],
        ),
        out_shape=blocks(count),
        cost_estimate=pl.CostEstimate(flops=0, bytes_accessed=4 << 20, transcendentals=0),
        compiler_params=pltpu.CompilerParams(vmem_limit_bytes=VMEM_LIMIT),
        name="pack",
    )(*(pltpu.with_memory_space_constraint(a, pltpu.HBM) for a in (lengths, queries, key_rows, value_rows)))


def attend_kernel(heads, part, q_at, out_at, from_pieces, to_pieces, lengths, place, q_ref, *refs):
    kv_refs, (out_ref, buffer, q_buf, out_buf, sems, q_sems, out_sems) = refs[: 2 * CHIPS], refs[-7:]
    step = pl.program_id(0)
    item, head_at = step % BINS, step // BINS
    ctx = place[0]
    chip, core = ctx // 2, ctx % 2
    prompt = lengths[item, 0]
    split = prompt + lengths[item, 1]
    end = split + lengths[item, 2]
    start = ctx * WIDTH
    factor = math.log2(math.e) / math.sqrt(HEAD)

    def active(w):
        if part is None:
            return True
        late = (core == 0) & ((w // BINS == 1) | (chip < CHIPS // 2))
        return late if part == "late" else jnp.logical_not(late)

    def copy(i, w):
        source = kv_refs[i].at[pl.ds(2 * (w // BINS), 2), w % BINS]
        return pltpu.make_async_copy(source, buffer.at[i, w], sems.at[i, w])

    def copy_q(w):
        b, h = w % BINS, w // BINS
        if from_pieces:
            source = q_ref.at[:, pl.ds(q_at + w * HALF, HALF)]
        else:
            column = q_at + h * GROUP * HEAD
            column = column if isinstance(column, int) else pl.multiple_of(column, GROUP * HEAD)
            source = q_ref.at[b, 0, :, pl.ds(column, GROUP * HEAD)]
        return pltpu.make_async_copy(source, q_buf.at[w], q_sems.at[w])

    def copy_out(w):
        if to_pieces:
            target = out_ref.at[:, pl.ds(out_at + w * HALF, HALF)]
        else:
            target = out_ref.at[w, 0, :, pl.ds(out_at, GROUP * HEAD)]
        return pltpu.make_async_copy(out_buf.at[w], target, out_sems.at[w])

    for w in range(heads * BINS):

        @pl.when((step == 0) & active(w))
        def _(w=w):
            copy_q(w).start()
            for i in range(2 * CHIPS):

                @pl.when(i // 2 <= chip)
                def _(i=i):
                    copy(i, w).start()

    working = active(step)

    @pl.when(working)
    def _():
        copy_q(step).wait()

    for i in range(2 * CHIPS):

        @pl.when(working & (i // 2 <= chip))
        def _(i=i):
            copy(i, step).wait()

    def read_head(head):
        if not from_pieces:
            return q_buf[step, :, pl.ds(head * HEAD, HEAD)]
        return jnp.concatenate([q_buf[step, 2 * r + head // HALF, head % HALF] for r in range(PARTS)], axis=0)

    def write_head(head, rows):
        if to_pieces:
            for r in range(PARTS):
                out_buf[step, 2 * r + head // HALF, head % HALF] = rows[r * PIECE : (r + 1) * PIECE]
        else:
            out_buf[step, :, pl.ds(head * HEAD, HEAD)] = rows

    def attend(chips):
        keys = jnp.concatenate([buffer[i, step, 0] for i in range(2 * chips)], axis=0)
        values = jnp.concatenate([buffer[i, step, 1] for i in range(2 * chips)], axis=0)
        t = start + lax.broadcasted_iota(jnp.int32, (WIDTH, WIDTH), 0)
        biases = []
        for i in range(2 * chips):
            origin = 2 * (chip - i // 2) + (core if i % 2 == 0 else 1 - core)
            u = origin * WIDTH + lax.broadcasted_iota(jnp.int32, (WIDTH, WIDTH), 1)
            hidden = (u > t) | ((t >= split) & (u >= prompt) & (u < split))
            biases.append(jnp.where(hidden, NEG, 0.0))
        bias = jnp.concatenate(biases, axis=1)
        live = (start + lax.broadcasted_iota(jnp.int32, (WIDTH, 1), 0)) < end
        bias = jnp.concatenate([bias, bias], axis=0)
        live = jnp.concatenate([live, live], axis=0)
        n = GROUP // 2
        qs = [jnp.concatenate([read_head(2 * i), read_head(2 * i + 1)], axis=0) for i in range(n)]
        scores = [lax.dot_general(q, keys, (((1,), (1,)), ((), ())), preferred_element_type=jnp.float32) + bias for q in qs]
        tops = [jnp.max(x, axis=1, keepdims=True) for x in scores]
        weights = [jnp.exp2((x - top) * factor) for x, top in zip(scores, tops)]
        wide = jnp.concatenate([values, jnp.ones_like(values)], axis=1)
        mixed = [jnp.dot(x.astype(BF16), wide, preferred_element_type=jnp.float32) for x in weights]
        for i in range(n):
            out = (mixed[i][:, :HEAD] * jnp.where(live, 1.0 / mixed[i][:, HEAD:], 0.0)).astype(BF16)
            write_head(2 * i, out[:WIDTH])
            write_head(2 * i + 1, out[WIDTH:])

    @pl.when(working & (end <= start))
    def _():
        out_buf[step] = jnp.zeros(out_buf.shape[1:], BF16)

    for chips in range(1, CHIPS + 1):

        @pl.when(working & (end > start) & (chip == chips - 1))
        def _(chips=chips):
            attend(chips)

    @pl.when(working)
    def _():
        copy_out(step).start()

    for w in range(heads * BINS):

        @pl.when((step == heads * BINS - 1) & active(w))
        def _(w=w):
            copy_out(w).wait()


def attend(lengths, place, q, q_at, kv, out_shape, out_at, name, from_pieces=False, to_pieces=True, into=None, heads=1, weight=1, part=None):
    hbm, anywhere = pl.BlockSpec(memory_space=pltpu.HBM), pl.BlockSpec(memory_space=pl.ANY)
    pairs = heads * BINS * GROUP * WIDTH * WIDTH * 2 * CHIPS
    steps = heads * BINS
    pieces, columns = (steps, ROWS, HALF, PIECE, HEAD), (steps, WIDTH, GROUP * HEAD)
    return pl.pallas_call(
        functools.partial(attend_kernel, heads, part, q_at, out_at, from_pieces, to_pieces),
        grid_spec=pltpu.PrefetchScalarGridSpec(
            num_scalar_prefetch=2,
            grid=(steps,),
            in_specs=[anywhere] * (1 + 2 * CHIPS) + [hbm] * (0 if into is None else 1),
            out_specs=hbm,
            scratch_shapes=[
                pltpu.VMEM((2 * CHIPS, steps, 2, WIDTH, HEAD), BF16),
                pltpu.VMEM(pieces if from_pieces else columns, BF16),
                pltpu.VMEM(pieces if to_pieces else columns, BF16),
                pltpu.SemaphoreType.DMA((2 * CHIPS, steps)),
                pltpu.SemaphoreType.DMA((steps,)),
                pltpu.SemaphoreType.DMA((steps,)),
            ],
        ),
        out_shape=out_shape,
        input_output_aliases={} if into is None else {3 + 2 * CHIPS: 0},
        cost_estimate=pl.CostEstimate(flops=int(weight * 20 * pairs * HEAD), bytes_accessed=4 << 20, transcendentals=pairs),
        compiler_params=pltpu.CompilerParams(vmem_limit_bytes=VMEM_LIMIT),
        name=name,
    )(
        pltpu.with_memory_space_constraint(lengths, pltpu.HBM),
        place,
        pltpu.with_memory_space_constraint(q, pltpu.VMEM if from_pieces else pltpu.HBM),
        *(pltpu.with_memory_space_constraint(piece, pltpu.VMEM) for piece in kv),
        *(() if into is None else (into,)),
    )


def forward_kernel(sizes, at, bin_of, r_ref, *refs):
    u_ref, u_buf, sems = refs[-3:]

    def leave(row):
        return pltpu.make_async_copy(u_buf.at[row], u_ref.at[row, pl.ds(at, u_buf.shape[1])], sems.at[row])

    for row in range(ROWS):
        for slot in range(BINS):
            b = bin_of[row * BINS + slot]
            base = 0
            for size in sizes:
                for n in range(size):
                    u_buf[row, base + slot * size + n] = r_ref[b // BINS, base + (b % BINS) * size + n]
                base += BINS * size
        leave(row).start()
    for row in range(ROWS):
        leave(row).wait()


def forward(bin_of, received, sizes, into, name):
    hbm = pl.BlockSpec(memory_space=pltpu.HBM)
    count = BINS * sum(sizes)
    at = 0 if into is None else into.shape[1] - count
    return pl.pallas_call(
        functools.partial(forward_kernel, sizes, at),
        grid_spec=pltpu.PrefetchScalarGridSpec(
            num_scalar_prefetch=1,
            grid=(),
            in_specs=[pl.BlockSpec(memory_space=pltpu.VMEM)] + [hbm] * (0 if into is None else 1),
            out_specs=hbm,
            scratch_shapes=[pltpu.VMEM((ROWS, count, PIECE, HEAD), BF16), pltpu.SemaphoreType.DMA((ROWS,))],
        ),
        out_shape=blocks(count) if into is None else blocks(into.shape[1]),
        input_output_aliases={} if into is None else {2: 0},
        cost_estimate=pl.CostEstimate(flops=0, bytes_accessed=4 << 20, transcendentals=0),
        compiler_params=pltpu.CompilerParams(vmem_limit_bytes=VMEM_LIMIT),
        name=name,
    )(bin_of, pltpu.with_memory_space_constraint(received, pltpu.VMEM), *(() if into is None else (into,)))


def place_kernel(at, column, r_ref, _, out_ref, out_buf, sems):
    heads = len(at)

    def leave(slot):
        columns = pl.ds(column, heads * GROUP * HEAD)
        return pltpu.make_async_copy(out_buf.at[slot], out_ref.at[slot, 0, :, columns], sems.at[slot])

    for slot in range(BINS):
        for j in range(ROWS):
            for n in range(HALF * heads):
                head = (n // HALF) * GROUP + (j % 2) * HALF + n % HALF
                rows, columns = pl.ds((j // 2) * PIECE, PIECE), pl.ds(head * HEAD, HEAD)
                out_buf[slot, rows, columns] = r_ref[j, at[n // HALF] + slot * HALF + n % HALF]
        leave(slot).start()
    for slot in range(BINS):
        leave(slot).wait()


def place(received, at, out, column, name):
    hbm = pl.BlockSpec(memory_space=pltpu.HBM)
    heads = len(at)
    return pl.pallas_call(
        functools.partial(place_kernel, at, column),
        in_specs=[pl.BlockSpec(memory_space=pltpu.VMEM), hbm],
        out_specs=hbm,
        out_shape=jax.ShapeDtypeStruct(out.shape, out.dtype),
        scratch_shapes=[
            pltpu.VMEM((BINS, WIDTH, heads * GROUP * HEAD), BF16),
            pltpu.SemaphoreType.DMA((BINS,)),
        ],
        input_output_aliases={1: 0},
        cost_estimate=pl.CostEstimate(flops=0, bytes_accessed=heads * (2 << 20), transcendentals=0),
        compiler_params=pltpu.CompilerParams(vmem_limit_bytes=VMEM_LIMIT),
        name=name,
    )(pltpu.with_memory_space_constraint(received, pltpu.VMEM), out)


def fetch(kv):
    pieces = [kv]
    for back in range(1, CHIPS):
        pairs = [(c, (c + 2 * back) % (2 * CHIPS)) for c in range(2 * CHIPS)]
        pieces.append(lax.ppermute(kv, "ctx", pairs))
    return pieces


def share(pieces):
    swap = [(c, c ^ 1) for c in range(2 * CHIPS)]
    return [p for piece in pieces for p in (piece, lax.ppermute(piece, "ctx", swap))]


def exchange(sent):
    return lax.all_to_all(sent, "dp", split_axis=0, concat_axis=0, tiled=True)


def shards(queries, key_rows, bin_value_rows, lengths, routes):
    my_row = lax.axis_index("dp")
    ctx = lax.axis_index("ctx").astype(jnp.int32)[None]
    flat = routes[:, 0]
    order = jnp.arange(ROWS * BINS, dtype=jnp.int32)
    earlier = (flat[:, None] == flat[None, :]) & (order[None, :] < order[:, None])
    slot = flat * BINS + jnp.sum(earlier.astype(jnp.int32), axis=1)
    bin_of = jnp.sum(jnp.where(slot[None, :] == order[:, None], order[None, :], 0), axis=1).astype(jnp.int32)

    def key_value(heads, near=None):
        k, v = key_rows, bin_value_rows
        if near is not None:
            k, v, near[CHIPS - 1] = lax.optimization_barrier((k, v, near[CHIPS - 1]))
        columns = [slice(head * HEAD, (head + 1) * HEAD) for head in heads]
        return jnp.stack([a[:, 0, :, c] for c in columns for a in (k, v)])

    wide = GROUP * HEAD

    near_1 = fetch(key_value([1]))
    got_1 = exchange(pack(lengths, queries, key_rows, bin_value_rows))
    near_23 = fetch(key_value([2, 3], near_1))

    second = attend(lengths, ctx, queries, wide, share(near_1), blocks(36), 0, "attend_1")
    second = forward(bin_of, got_1, (HALF, 1), second, "forward_0")
    got_2 = exchange(second)
    near_23[1:], _ = lax.optimization_barrier((near_23[1:], second))

    digits = got_1[:, 5 * BINS, 0, : 6 * BINS].astype(jnp.float32).astype(jnp.int32)
    all_lengths = (digits[:, : 3 * BINS] * 32 + digits[:, 3 * BINS :]).reshape(ROWS * BINS, 3)
    my_bins = lax.dynamic_slice_in_dim(bin_of, my_row * BINS, BINS)
    slot_lengths = jnp.sum(jnp.where(my_bins[:, None, None] == order[None, :, None], all_lengths[None], 0), axis=1).astype(jnp.int32)

    pieces_23 = share(near_23)
    third = attend(lengths, ctx, queries, 2 * wide, pieces_23, blocks(48), 0, "attend_23_early", heads=2, weight=3, part="early")
    third, got_2 = lax.optimization_barrier((third, got_2))
    third = attend(lengths, ctx, queries, 2 * wide, pieces_23, blocks(48), 0, "attend_23_late", heads=2, part="late", into=third)
    third = forward(bin_of, got_2, (HALF,), third, "forward_1")
    third, slot_lengths = lax.optimization_barrier((third, slot_lengths))
    got_3 = exchange(third)

    kv_0 = jnp.transpose(got_2[:, 32:].reshape(PARTS, 2, BINS, PIECE, HEAD), (1, 2, 0, 3, 4))
    pieces_0 = share(fetch(kv_0.reshape(2, BINS, WIDTH, HEAD)))
    full = pltpu.HBM(queries.shape, BF16)

    fourth = forward(bin_of, got_3, (HALF, HALF), None, "forward_23")
    fourth, pieces_0 = lax.optimization_barrier((fourth, pieces_0))
    got_4 = exchange(fourth)
    out = attend(slot_lengths, ctx, got_2, 4 * HALF, pieces_0, full, 0, "attend_0", True, False)
    out = place(got_3, (32,), out, GROUP * HEAD, "place_1")
    return place(got_4, (0, 16), out, 2 * GROUP * HEAD, "place_23")


def solution(mesh):
    in_specs = (
        P("dp", "ctx", None, None),
        P("dp", "ctx", None, None),
        P("dp", "ctx", None, None),
        P("dp", None),
        P(),
    )
    out_specs = P("dp", "ctx", None, None)
    return jax.shard_map(shards, mesh=mesh, in_specs=in_specs, out_specs=out_specs, check_vma=False)
```

```python
import functools
import math

import jax
import jax.numpy as jnp
from jax import lax
from jax.experimental import pallas as pl
from jax.experimental.pallas import tpu as pltpu
from jax.sharding import PartitionSpec as P

BINS = 4
ROWS = 16
CHIPS = 4
WIDTH = 128
HEAD = 128
GROUP = 8
PIECE = 16
PARTS = WIDTH // PIECE
HALF = GROUP // 2
NEG = -1e30
BF16 = jnp.bfloat16
VMEM_LIMIT = 40 << 20


def blocks(count):
    return pltpu.HBM((ROWS, count, PIECE, HEAD), BF16)


def pack_kernel(lengths, q_ref, k_ref, v_ref, u_ref, q_buf, k_buf, v_buf, u_buf, in_sems, out_sems):
    def arrive(b):
        wide, narrow = pl.ds(0, GROUP * HEAD), pl.ds(0, HEAD)
        return [
            pltpu.make_async_copy(q_ref.at[b, 0, :, wide], q_buf.at[b], in_sems.at[0, b]),
            pltpu.make_async_copy(k_ref.at[b, 0, :, narrow], k_buf.at[b], in_sems.at[1, b]),
            pltpu.make_async_copy(v_ref.at[b, 0, :, narrow], v_buf.at[b], in_sems.at[2, b]),
        ]

    def leave(i):
        part = pl.ds(i * HALF, HALF if i < BINS else BINS + 1)
        return pltpu.make_async_copy(u_buf.at[:, part], u_ref.at[:, part], out_sems.at[i])

    for b in range(BINS):
        for copy in arrive(b):
            copy.start()
    lane = lax.broadcasted_iota(jnp.int32, (PIECE, HEAD), 1)
    digits = jnp.zeros((PIECE, HEAD), jnp.int32)
    for i in range(3 * BINS):
        length = lengths[i // 3, i % 3]
        digits = jnp.where(lane == i, length // 32, digits)
        digits = jnp.where(lane == 3 * BINS + i, length % 32, digits)
    digits = digits.astype(jnp.float32).astype(BF16)
    for b in range(BINS):
        for copy in arrive(b):
            copy.wait()
        for j in range(ROWS):
            rows = pl.ds((j // 2) * PIECE, PIECE)
            for n in range(HALF):
                u_buf[j, b * HALF + n] = q_buf[b, rows, pl.ds(((j % 2) * HALF + n) * HEAD, HEAD)]
            u_buf[j, BINS * HALF + b] = (k_buf if j % 2 == 0 else v_buf)[b, rows]
            if b == 0:
                u_buf[j, BINS * HALF + BINS] = digits
        leave(b).start()
    leave(BINS).start()
    for i in range(BINS + 1):
        leave(i).wait()


def pack(lengths, queries, key_rows, value_rows):
    hbm = pl.BlockSpec(memory_space=pltpu.HBM)
    count = BINS * HALF + BINS + 1
    return pl.pallas_call(
        pack_kernel,
        grid_spec=pltpu.PrefetchScalarGridSpec(
            num_scalar_prefetch=1,
            grid=(),
            in_specs=[hbm] * 3,
            out_specs=hbm,
            scratch_shapes=[
                pltpu.VMEM((BINS, WIDTH, GROUP * HEAD), BF16),
                pltpu.VMEM((BINS, WIDTH, HEAD), BF16),
                pltpu.VMEM((BINS, WIDTH, HEAD), BF16),
                pltpu.VMEM((ROWS, count, PIECE, HEAD), BF16),
                pltpu.SemaphoreType.DMA((3, BINS)),
                pltpu.SemaphoreType.DMA((BINS + 1,)),
            ],
        ),
        out_shape=blocks(count),
        cost_estimate=pl.CostEstimate(flops=0, bytes_accessed=4 << 20, transcendentals=0),
        compiler_params=pltpu.CompilerParams(vmem_limit_bytes=VMEM_LIMIT),
        name="pack",
    )(*(pltpu.with_memory_space_constraint(a, pltpu.HBM) for a in (lengths, queries, key_rows, value_rows)))


def attend_kernel(heads, part, q_at, out_at, from_pieces, to_pieces, lengths, place, q_ref, *refs):
    kv_refs, (out_ref, buffer, q_buf, out_buf, sems, q_sems, out_sems) = refs[: 2 * CHIPS], refs[-7:]
    step = pl.program_id(0)
    item, head_at = step % BINS, step // BINS
    ctx = place[0]
    chip, core = ctx // 2, ctx % 2
    prompt = lengths[item, 0]
    split = prompt + lengths[item, 1]
    end = split + lengths[item, 2]
    start = ctx * WIDTH
    factor = math.log2(math.e) / math.sqrt(HEAD)

    def active(w):
        if part is None:
            return True
        late = (core == 0) & (((w // BINS == 1) & (w % BINS >= 1)) | (chip < CHIPS // 2))
        return late if part == "late" else jnp.logical_not(late)

    def copy(i, w):
        source = kv_refs[i].at[pl.ds(2 * (w // BINS), 2), w % BINS]
        return pltpu.make_async_copy(source, buffer.at[i, w], sems.at[i, w])

    def copy_q(w):
        b, h = w % BINS, w // BINS
        if from_pieces:
            source = q_ref.at[:, pl.ds(q_at + w * HALF, HALF)]
        else:
            column = q_at + h * GROUP * HEAD
            column = column if isinstance(column, int) else pl.multiple_of(column, GROUP * HEAD)
            source = q_ref.at[b, 0, :, pl.ds(column, GROUP * HEAD)]
        return pltpu.make_async_copy(source, q_buf.at[w], q_sems.at[w])

    def copy_out(w):
        if to_pieces:
            target = out_ref.at[:, pl.ds(out_at + w * HALF, HALF)]
        else:
            target = out_ref.at[w, 0, :, pl.ds(out_at, GROUP * HEAD)]
        return pltpu.make_async_copy(out_buf.at[w], target, out_sems.at[w])

    for w in range(heads * BINS):

        @pl.when((step == 0) & active(w))
        def _(w=w):
            copy_q(w).start()
            for i in range(2 * CHIPS):

                @pl.when(i // 2 <= chip)
                def _(i=i):
                    copy(i, w).start()

    working = active(step)

    @pl.when(working)
    def _():
        copy_q(step).wait()

    for i in range(2 * CHIPS):

        @pl.when(working & (i // 2 <= chip))
        def _(i=i):
            copy(i, step).wait()

    def read_head(head):
        if not from_pieces:
            return q_buf[step, :, pl.ds(head * HEAD, HEAD)]
        return jnp.concatenate([q_buf[step, 2 * r + head // HALF, head % HALF] for r in range(PARTS)], axis=0)

    def write_head(head, rows):
        if to_pieces:
            for r in range(PARTS):
                out_buf[step, 2 * r + head // HALF, head % HALF] = rows[r * PIECE : (r + 1) * PIECE]
        else:
            out_buf[step, :, pl.ds(head * HEAD, HEAD)] = rows

    def attend(chips):
        keys = jnp.concatenate([buffer[i, step, 0] for i in range(2 * chips)], axis=0)
        values = jnp.concatenate([buffer[i, step, 1] for i in range(2 * chips)], axis=0)
        t = start + lax.broadcasted_iota(jnp.int32, (WIDTH, WIDTH), 0)
        biases = []
        for i in range(2 * chips):
            origin = 2 * (chip - i // 2) + (core if i % 2 == 0 else 1 - core)
            u = origin * WIDTH + lax.broadcasted_iota(jnp.int32, (WIDTH, WIDTH), 1)
            hidden = (u > t) | ((t >= split) & (u >= prompt) & (u < split))
            biases.append(jnp.where(hidden, NEG, 0.0))
        bias = jnp.concatenate(biases, axis=1)
        live = (start + lax.broadcasted_iota(jnp.int32, (WIDTH, 1), 0)) < end
        bias = jnp.concatenate([bias, bias], axis=0)
        live = jnp.concatenate([live, live], axis=0)
        n = GROUP // 2
        qs = [jnp.concatenate([read_head(2 * i), read_head(2 * i + 1)], axis=0) for i in range(n)]
        scores = [lax.dot_general(q, keys, (((1,), (1,)), ((), ())), preferred_element_type=jnp.float32) + bias for q in qs]
        tops = [jnp.max(x, axis=1, keepdims=True) for x in scores]
        weights = [jnp.exp2((x - top) * factor) for x, top in zip(scores, tops)]
        wide = jnp.concatenate([values, jnp.ones_like(values)], axis=1)
        mixed = [jnp.dot(x.astype(BF16), wide, preferred_element_type=jnp.float32) for x in weights]
        for i in range(n):
            out = (mixed[i][:, :HEAD] * jnp.where(live, 1.0 / mixed[i][:, HEAD:], 0.0)).astype(BF16)
            write_head(2 * i, out[:WIDTH])
            write_head(2 * i + 1, out[WIDTH:])

    @pl.when(working & (end <= start))
    def _():
        out_buf[step] = jnp.zeros(out_buf.shape[1:], BF16)

    for chips in range(1, CHIPS + 1):

        @pl.when(working & (end > start) & (chip == chips - 1))
        def _(chips=chips):
            attend(chips)

    @pl.when(working)
    def _():
        copy_out(step).start()

    for w in range(heads * BINS):

        @pl.when((step == heads * BINS - 1) & active(w))
        def _(w=w):
            copy_out(w).wait()


def attend(lengths, place, q, q_at, kv, out_shape, out_at, name, from_pieces=False, to_pieces=True, into=None, heads=1, weight=1, part=None):
    hbm, anywhere = pl.BlockSpec(memory_space=pltpu.HBM), pl.BlockSpec(memory_space=pl.ANY)
    pairs = heads * BINS * GROUP * WIDTH * WIDTH * 2 * CHIPS
    steps = heads * BINS
    pieces, columns = (steps, ROWS, HALF, PIECE, HEAD), (steps, WIDTH, GROUP * HEAD)
    return pl.pallas_call(
        functools.partial(attend_kernel, heads, part, q_at, out_at, from_pieces, to_pieces),
        grid_spec=pltpu.PrefetchScalarGridSpec(
            num_scalar_prefetch=2,
            grid=(steps,),
            in_specs=[anywhere] * (1 + 2 * CHIPS) + [hbm] * (0 if into is None else 1),
            out_specs=hbm,
            scratch_shapes=[
                pltpu.VMEM((2 * CHIPS, steps, 2, WIDTH, HEAD), BF16),
                pltpu.VMEM(pieces if from_pieces else columns, BF16),
                pltpu.VMEM(pieces if to_pieces else columns, BF16),
                pltpu.SemaphoreType.DMA((2 * CHIPS, steps)),
                pltpu.SemaphoreType.DMA((steps,)),
                pltpu.SemaphoreType.DMA((steps,)),
            ],
        ),
        out_shape=out_shape,
        input_output_aliases={} if into is None else {3 + 2 * CHIPS: 0},
        cost_estimate=pl.CostEstimate(flops=int(weight * 20 * pairs * HEAD), bytes_accessed=4 << 20, transcendentals=pairs),
        compiler_params=pltpu.CompilerParams(vmem_limit_bytes=VMEM_LIMIT),
        name=name,
    )(
        pltpu.with_memory_space_constraint(lengths, pltpu.HBM),
        place,
        pltpu.with_memory_space_constraint(q, pltpu.VMEM if from_pieces else pltpu.HBM),
        *(pltpu.with_memory_space_constraint(piece, pltpu.VMEM) for piece in kv),
        *(() if into is None else (into,)),
    )


def forward_kernel(sizes, at, bin_of, r_ref, *refs):
    u_ref, u_buf, sems = refs[-3:]

    def leave(row):
        return pltpu.make_async_copy(u_buf.at[row], u_ref.at[row, pl.ds(at, u_buf.shape[1])], sems.at[row])

    for row in range(ROWS):
        for slot in range(BINS):
            b = bin_of[row * BINS + slot]
            base = 0
            for size in sizes:
                for n in range(size):
                    u_buf[row, base + slot * size + n] = r_ref[b // BINS, base + (b % BINS) * size + n]
                base += BINS * size
        leave(row).start()
    for row in range(ROWS):
        leave(row).wait()


def forward(bin_of, received, sizes, into, name):
    hbm = pl.BlockSpec(memory_space=pltpu.HBM)
    count = BINS * sum(sizes)
    at = 0 if into is None else into.shape[1] - count
    return pl.pallas_call(
        functools.partial(forward_kernel, sizes, at),
        grid_spec=pltpu.PrefetchScalarGridSpec(
            num_scalar_prefetch=1,
            grid=(),
            in_specs=[pl.BlockSpec(memory_space=pltpu.VMEM)] + [hbm] * (0 if into is None else 1),
            out_specs=hbm,
            scratch_shapes=[pltpu.VMEM((ROWS, count, PIECE, HEAD), BF16), pltpu.SemaphoreType.DMA((ROWS,))],
        ),
        out_shape=blocks(count) if into is None else blocks(into.shape[1]),
        input_output_aliases={} if into is None else {2: 0},
        cost_estimate=pl.CostEstimate(flops=0, bytes_accessed=4 << 20, transcendentals=0),
        compiler_params=pltpu.CompilerParams(vmem_limit_bytes=VMEM_LIMIT),
        name=name,
    )(bin_of, pltpu.with_memory_space_constraint(received, pltpu.VMEM), *(() if into is None else (into,)))


def place_kernel(at, column, r_ref, _, out_ref, out_buf, sems):
    heads = len(at)

    def leave(slot):
        columns = pl.ds(column, heads * GROUP * HEAD)
        return pltpu.make_async_copy(out_buf.at[slot], out_ref.at[slot, 0, :, columns], sems.at[slot])

    for slot in range(BINS):
        for j in range(ROWS):
            for n in range(HALF * heads):
                head = (n // HALF) * GROUP + (j % 2) * HALF + n % HALF
                rows, columns = pl.ds((j // 2) * PIECE, PIECE), pl.ds(head * HEAD, HEAD)
                out_buf[slot, rows, columns] = r_ref[j, at[n // HALF] + slot * HALF + n % HALF]
        leave(slot).start()
    for slot in range(BINS):
        leave(slot).wait()


def place(received, at, out, column, name):
    hbm = pl.BlockSpec(memory_space=pltpu.HBM)
    heads = len(at)
    return pl.pallas_call(
        functools.partial(place_kernel, at, column),
        in_specs=[pl.BlockSpec(memory_space=pltpu.VMEM), hbm],
        out_specs=hbm,
        out_shape=jax.ShapeDtypeStruct(out.shape, out.dtype),
        scratch_shapes=[
            pltpu.VMEM((BINS, WIDTH, heads * GROUP * HEAD), BF16),
            pltpu.SemaphoreType.DMA((BINS,)),
        ],
        input_output_aliases={1: 0},
        cost_estimate=pl.CostEstimate(flops=0, bytes_accessed=heads * (2 << 20), transcendentals=0),
        compiler_params=pltpu.CompilerParams(vmem_limit_bytes=VMEM_LIMIT),
        name=name,
    )(pltpu.with_memory_space_constraint(received, pltpu.VMEM), out)


def fetch(kv):
    pieces = [kv]
    for back in range(1, CHIPS):
        pairs = [(c, (c + 2 * back) % (2 * CHIPS)) for c in range(2 * CHIPS)]
        pieces.append(lax.ppermute(kv, "ctx", pairs))
    return pieces


def share(pieces):
    swap = [(c, c ^ 1) for c in range(2 * CHIPS)]
    return [p for piece in pieces for p in (piece, lax.ppermute(piece, "ctx", swap))]


def exchange(sent):
    return lax.all_to_all(sent, "dp", split_axis=0, concat_axis=0, tiled=True)


def shards(queries, key_rows, bin_value_rows, lengths, routes):
    my_row = lax.axis_index("dp")
    ctx = lax.axis_index("ctx").astype(jnp.int32)[None]
    flat = routes[:, 0]
    order = jnp.arange(ROWS * BINS, dtype=jnp.int32)
    earlier = (flat[:, None] == flat[None, :]) & (order[None, :] < order[:, None])
    slot = flat * BINS + jnp.sum(earlier.astype(jnp.int32), axis=1)
    bin_of = jnp.sum(jnp.where(slot[None, :] == order[:, None], order[None, :], 0), axis=1).astype(jnp.int32)

    def key_value(heads, near=None):
        k, v = key_rows, bin_value_rows
        if near is not None:
            k, v, near[CHIPS - 1] = lax.optimization_barrier((k, v, near[CHIPS - 1]))
        columns = [slice(head * HEAD, (head + 1) * HEAD) for head in heads]
        return jnp.stack([a[:, 0, :, c] for c in columns for a in (k, v)])

    wide = GROUP * HEAD

    near_1 = fetch(key_value([1]))
    got_1 = exchange(pack(lengths, queries, key_rows, bin_value_rows))
    near_23 = fetch(key_value([2, 3], near_1))

    second = attend(lengths, ctx, queries, wide, share(near_1), blocks(36), 0, "attend_1")
    second = forward(bin_of, got_1, (HALF, 1), second, "forward_0")
    got_2 = exchange(second)
    near_23[1:], _ = lax.optimization_barrier((near_23[1:], second))

    digits = got_1[:, 5 * BINS, 0, : 6 * BINS].astype(jnp.float32).astype(jnp.int32)
    all_lengths = (digits[:, : 3 * BINS] * 32 + digits[:, 3 * BINS :]).reshape(ROWS * BINS, 3)
    my_bins = lax.dynamic_slice_in_dim(bin_of, my_row * BINS, BINS)
    slot_lengths = jnp.sum(jnp.where(my_bins[:, None, None] == order[None, :, None], all_lengths[None], 0), axis=1).astype(jnp.int32)

    pieces_23 = share(near_23)
    third = attend(lengths, ctx, queries, 2 * wide, pieces_23, blocks(48), 0, "attend_23_early", heads=2, weight=3, part="early")
    third, got_2 = lax.optimization_barrier((third, got_2))
    third = attend(lengths, ctx, queries, 2 * wide, pieces_23, blocks(48), 0, "attend_23_late", heads=2, part="late", into=third)
    third = forward(bin_of, got_2, (HALF,), third, "forward_1")
    third, slot_lengths = lax.optimization_barrier((third, slot_lengths))
    got_3 = exchange(third)

    kv_0 = jnp.transpose(got_2[:, 32:].reshape(PARTS, 2, BINS, PIECE, HEAD), (1, 2, 0, 3, 4))
    pieces_0 = share(fetch(kv_0.reshape(2, BINS, WIDTH, HEAD)))
    full = pltpu.HBM(queries.shape, BF16)

    fourth = forward(bin_of, got_3, (HALF, HALF), None, "forward_23")
    fourth, pieces_0 = lax.optimization_barrier((fourth, pieces_0))
    got_4 = exchange(fourth)
    out = attend(slot_lengths, ctx, got_2, 4 * HALF, pieces_0, full, 0, "attend_0", True, False)
    out = place(got_3, (32,), out, GROUP * HEAD, "place_1")
    return place(got_4, (0, 16), out, 2 * GROUP * HEAD, "place_23")


def solution(mesh):
    in_specs = (
        P("dp", "ctx", None, None),
        P("dp", "ctx", None, None),
        P("dp", "ctx", None, None),
        P("dp", None),
        P(),
    )
    out_specs = P("dp", "ctx", None, None)
    return jax.shard_map(shards, mesh=mesh, in_specs=in_specs, out_specs=out_specs, check_vma=False)
```
